256 devices in a mesh: dp: 16 (over z, y_lo), feat: 16 (over y_hi, x, core).
Axes of the slice: x: 4, y: 4 (y_hi: 2, y_lo: 2; y = y_hi * 2 + y_lo), z: 8, core: 2. Of those that a mesh axis runs over, the one named last changes fastest.
Arguments:
- first_view: bfloat16 [4096, 16384], P('dp', 'feat')
- second_view: bfloat16 [4096, 16384], P('dp', 'feat')
Outputs:
- first_grad: float32 [4096, 16384], P('dp', 'feat')
- second_grad: float32 [4096, 16384], P('dp', 'feat')
- loss_value: float32 [], replicated
All inputs are finite; a program needn't handle non-finite values.
Results may differ from the reference program's by a relative error of at most 0.0029.
Values may be sent and summed in bfloat16 or wider, within the bound.
No kernel may reach another device: no remote copies, remote signals or barrier semaphores. Data moves between devices by JAX's collectives and lax.ppermute only.
A program may use at most 128 MiB of HBM per device.

```python
import jax
import jax.numpy as jnp

FEATURES = 16384
BATCH = 4096


def common_views(key, strength):
    base_key = jax.random.fold_in(key, 0)
    off_key = jax.random.fold_in(key, 3)
    factor_key = jax.random.fold_in(key, 4)
    loading_key = jax.random.fold_in(key, 5)
    base = jax.random.normal(base_key, (BATCH, FEATURES), jnp.float32)
    factors = jax.random.normal(factor_key, (4, BATCH), jnp.float32)
    loadings = jax.random.normal(loading_key, (4, FEATURES), jnp.float32)
    for index in range(4):
        base = base + strength * factors[index][:, None] * loadings[index][None, :]
    row_ramp = 0.75 + 0.55 * jnp.arange(BATCH, dtype=jnp.float32) / (BATCH - 1)
    col_ramp = 0.75 + 0.55 * jnp.arange(FEATURES, dtype=jnp.float32) / (FEATURES - 1)
    row_scale = row_ramp
    col_scale = col_ramp
    offset = jax.random.uniform(off_key, (FEATURES,), jnp.float32, -1.0, 1.0)
    return (base, row_scale[:, None] * col_scale[None, :], offset)


def draw_first_view(key, part):
    strength = 0.05
    base, scaling, offset = common_views(key, strength)
    key = jax.random.fold_in(key, 41)
    noise = jax.random.normal(key, (BATCH, FEATURES), jnp.float32)
    return ((base + 0.6 * noise) * scaling + offset).astype(jnp.bfloat16)


def draw_second_view(key, part):
    strength = 0.05
    base, scaling, offset = common_views(key, strength)
    key = jax.random.fold_in(key, 53)
    noise = jax.random.normal(key, (BATCH, FEATURES), jnp.float32)
    return ((base + 0.6 * noise) * scaling + 0.5 * offset).astype(jnp.bfloat16)


def setup_inputs(seed: int = 0) -> dict:
    streams_of = jax.random.split(jax.random.key(seed), 3)
    first_view = draw_first_view(jax.random.fold_in(streams_of[2], 71), 0)
    second_view = draw_second_view(jax.random.fold_in(streams_of[2], 71), 0)
    return dict(first_view=first_view, second_view=second_view)


def reference(first_view, second_view):
    batch_size, feature_count = first_view.shape
    float_a = first_view.astype(jnp.float32)
    float_b = second_view.astype(jnp.float32)
    mean_a = jnp.sum(float_a, axis=0) / batch_size
    mean_b = jnp.sum(float_b, axis=0) / batch_size
    cent_a = (float_a - mean_a).astype(jnp.bfloat16)
    cent_b = (float_b - mean_b).astype(jnp.bfloat16)
    var_a = jnp.sum(jnp.square(cent_a.astype(jnp.float32)), axis=0) / (batch_size - 1)
    var_b = jnp.sum(jnp.square(cent_b.astype(jnp.float32)), axis=0) / (batch_size - 1)
    gram_a = jnp.dot(cent_a, cent_a.T, preferred_element_type=jnp.float32)
    gram_b = jnp.dot(cent_b, cent_b.T, preferred_element_type=jnp.float32)
    differ = float_a - float_b
    invariance = jnp.sum(differ * differ) / (batch_size * feature_count)
    denominator = (batch_size - 1.0) ** 2
    cov_a = (jnp.sum(gram_a * gram_a) / denominator - jnp.sum(var_a * var_a)) / feature_count
    cov_b = (jnp.sum(gram_b * gram_b) / denominator - jnp.sum(var_b * var_b)) / feature_count
    loss_value = 25.0 * invariance + cov_a + cov_b
    weight = 12.5 * (batch_size - 1.0) / batch_size
    prod_a = jnp.dot(gram_a.astype(jnp.bfloat16), cent_a, preferred_element_type=jnp.float32)
    prod_b = jnp.dot(gram_b.astype(jnp.bfloat16), cent_b, preferred_element_type=jnp.float32)
    first_grad = prod_a / (batch_size - 1.0) - cent_a.astype(jnp.float32) * var_a + weight * differ
    second_grad = prod_b / (batch_size - 1.0) - cent_b.astype(jnp.float32) * var_b - weight * differ
    return first_grad, second_grad, loss_value
```

```python
import jax
import jax.numpy as jnp
from jax import lax
from jax.sharding import Mesh, PartitionSpec as P

AXES = ("z", "yl", "yh", "x", "core")
SIZES = (8, 2, 2, 4, 2)
F32, BF16 = jnp.float32, jnp.bfloat16


def shift(value, axis, step):
    size = lax.axis_size(axis)
    return lax.ppermute(value, axis, [(i, (i + step) % size) for i in range(size)])


def swap(value, axis, bit):
    size = lax.axis_size(axis)
    return lax.ppermute(value, axis, [(i, i ^ bit) for i in range(size)])


def dot_t(left, right):
    return lax.dot_general(left, right, (((1,), (1,)), ((), ())), preferred_element_type=F32)


def reduce_gram(part):
    rows, cols = part.shape
    blocks = part.astype(BF16).reshape(8, rows // 8, cols)
    got = lax.all_to_all(blocks, ("yh", "x"), 0, 0, tiled=True)
    total = jnp.sum(got.astype(F32), axis=0)
    square = jnp.sum(total * total)
    out = jnp.broadcast_to(total.astype(BF16)[None], (8, rows // 8, cols))
    whole = lax.all_to_all(out, ("yh", "x"), 0, 0, tiled=True)
    return whole.reshape(rows, cols), square


def per_device(first_view, second_view):
    rows, feats = first_view.shape
    batch = rows * 16
    total_feats = feats * 16
    is_zero = lax.axis_index("core") == 0
    own = jnp.where(is_zero, first_view, second_view)
    give = jnp.where(is_zero, second_view, first_view)
    raw = jnp.concatenate([own, swap(give, "core", 1)], axis=1)

    up1, dn1 = shift(raw, "z", 1), shift(raw, "z", -1)
    other = swap(raw, "yl", 1)

    sums = jnp.sum(raw.astype(F32), axis=0, keepdims=True)
    sums = sums + swap(sums, "yl", 1)
    for bit in (1, 2, 4):
        sums = sums + swap(sums, "z", bit)
    mean = sums / batch

    up2, dn2 = shift(up1, "z", 1), shift(dn1, "z", -1)
    up3, dn3 = shift(up2, "z", 1), shift(dn2, "z", -1)
    half = rows // 2
    far = jnp.concatenate([shift(up3[:half], "z", 1), shift(dn3[half:], "z", -1)], axis=0)

    def center(value):
        return (value.astype(F32) - mean).astype(BF16)

    mine = center(raw)
    left = jnp.concatenate([mine, center(other)], axis=0)
    group_a = jnp.concatenate([mine, center(up1), center(dn1), center(up2), center(dn2)], axis=0)
    group_b = jnp.concatenate([center(up3), center(dn3), center(far)], axis=0)
    gram_a, square_a = reduce_gram(dot_t(left, group_a))
    gram_b, square_b = reduce_gram(dot_t(left, group_b))

    squares = jnp.sum(jnp.square(group_a.astype(F32)), axis=0, keepdims=True) + jnp.sum(
        jnp.square(group_b.astype(F32)), axis=0, keepdims=True
    )
    var = (squares + swap(squares, "yl", 1)) / (batch - 1)

    differ = first_view.astype(F32) - second_view.astype(F32)
    first_dp = (lax.axis_index("z") == 0) & (lax.axis_index("yl") == 0)
    first_feat = first_dp
    var_sq = jnp.where(first_feat, jnp.sum(var * var), F32(0.0))
    loss = (
        25.0 * jnp.sum(differ * differ) / (batch * total_feats)
        + ((square_a + square_b) / (batch - 1.0) ** 2 - var_sq) / total_feats
    )
    loss = jnp.full((1, 128), loss, F32)
    for axis, bit in (("core", 1), ("x", 1), ("x", 2), ("yl", 1), ("z", 1), ("yh", 1), ("z", 2), ("z", 4)):
        loss = loss + swap(loss, axis, bit)

    def product(lo):
        return jnp.dot(gram_a[lo : lo + rows], group_a, preferred_element_type=F32) + jnp.dot(
            gram_b[lo : lo + rows], group_b, preferred_element_type=F32
        )

    away = swap(product(rows).astype(BF16), "yl", 1)
    prod = product(0) + away.astype(F32)
    term = prod / (batch - 1.0) - mine.astype(F32) * var
    got = swap(term[:, feats:], "core", 1)
    weight = 12.5 * (batch - 1.0) / batch
    kept = term[:, :feats]
    first_grad = jnp.where(is_zero, kept, got) + weight * differ
    second_grad = jnp.where(is_zero, got, kept) - weight * differ
    return first_grad, second_grad, loss[0, 0]


def solution(mesh):
    fine = Mesh(mesh.devices.reshape(SIZES), AXES)
    spec = P(("z", "yl"), ("yh", "x", "core"))
    return jax.shard_map(
        per_device,
        mesh=fine,
        in_specs=(spec, spec),
        out_specs=(spec, spec, P()),
        check_vma=False,
    )
```

```python
import jax
import jax.numpy as jnp
from jax import lax
from jax.sharding import Mesh, PartitionSpec as P

AXES = ("z", "yl", "yh", "x", "core")
SIZES = (8, 2, 2, 4, 2)
F32, BF16 = jnp.float32, jnp.bfloat16


def shift(value, axis, step):
    size = lax.axis_size(axis)
    return lax.ppermute(value, axis, [(i, (i + step) % size) for i in range(size)])


def swap(value, axis, bit):
    size = lax.axis_size(axis)
    return lax.ppermute(value, axis, [(i, i ^ bit) for i in range(size)])


def tie(*values):
    return lax.optimization_barrier(values)


def dot_t(left, right):
    return lax.dot_general(left, right, (((1,), (1,)), ((), ())), preferred_element_type=F32)


def send_x(part):
    block = part.shape[0] // 4
    rounded = part[block:].astype(BF16)
    return [shift(rounded[block * (k - 1) : block * k], "x", k) for k in (1, 2, 3)]


def add_x(part, got):
    total = part[: part.shape[0] // 4]
    for value in got:
        total = total + value.astype(F32)
    return total


def spread_x(total):
    rounded = total.astype(BF16)
    return [rounded] + [shift(rounded, "x", -k) for k in (1, 2, 3)]


def swap_both(value):
    pairs = [(i, i ^ 3) for i in range(4)]
    return lax.ppermute(value, ("yl", "core"), pairs)


def per_device(first_view, second_view):
    rows, feats = first_view.shape
    batch = rows * 16
    total_feats = feats * 16
    half = rows // 2
    is_zero = lax.axis_index("core") == 0
    x_at = lax.axis_index("x")
    own = jnp.where(is_zero, first_view, second_view)
    give = jnp.where(is_zero, second_view, first_view)
    raw = jnp.concatenate([own, swap(give, "core", 1)], axis=1)

    up1, dn1 = shift(raw, "z", 1), shift(raw, "z", -1)
    other = swap(raw, "yl", 1)
    sums = jnp.sum(raw.astype(F32), axis=0, keepdims=True)
    every = lax.all_to_all(jnp.broadcast_to(sums[None], (16, 1, 2 * feats)), ("z", "yl"), 0, 0, tiled=True)
    mean = jnp.sum(every, axis=0) / batch
    up1, dn1, mean = tie(up1, dn1, mean)

    def center(value):
        return (value.astype(F32) - mean).astype(BF16)

    def centers(*values):
        return jnp.concatenate([center(v) for v in values], axis=0)

    up2, dn2 = shift(up1, "z", 1), shift(dn1, "z", -1)
    mine = center(raw)
    left = jnp.concatenate([mine, center(other)], axis=0)
    turned = lax.dynamic_slice_in_dim(jnp.concatenate([left, left], axis=0), x_at * half, 2 * rows, 0)
    cols_a = jnp.concatenate([mine, centers(up1, dn1)], axis=0)
    part_a = dot_t(turned, cols_a)
    got_a = send_x(part_a)
    up2, dn2, *got_a = tie(up2, dn2, *got_a)

    up3, dn3 = shift(up2, "z", 1), shift(dn2, "z", -1)
    total_a = add_x(part_a, got_a)
    total_a = total_a + swap(total_a.astype(BF16), "yh", 1).astype(F32)
    gram_a = spread_x(total_a)
    cols_b = centers(up2, dn2)
    part_b = dot_t(turned, cols_b)
    got_b = send_x(part_b)
    up3, dn3, *both = tie(up3, dn3, *gram_a, *got_b)
    gram_a, got_b = both[:4], both[4:]

    far_a, far_b = shift(up3[:half], "z", 1), shift(dn3[half:], "z", -1)
    total_b = add_x(part_b, got_b)
    total_b = total_b + swap(total_b.astype(BF16), "yh", 1).astype(F32)
    cols_c = centers(up3, dn3)
    part_c = dot_t(turned, cols_c)
    got_c = send_x(part_c)
    far_a, far_b, total_b, *got_c = tie(far_a, far_b, total_b, *got_c)

    cols_d = centers(far_a, far_b)
    part_d = dot_t(turned, cols_d)
    got_d = send_x(part_d)
    gram_b = spread_x(total_b)
    total_c = add_x(part_c, got_c)
    total_c, *got_d = tie(total_c, *got_d)

    total_c = jnp.concatenate([total_c, add_x(part_d, got_d)], axis=1)
    cross_c = swap(total_c.astype(BF16), "yh", 1)
    squares = sum(jnp.sum(jnp.square(c.astype(F32)), axis=0, keepdims=True) for c in (cols_a, cols_b, cols_c, cols_d))
    var = (squares + swap(squares, "yl", 1)) / (batch - 1)
    cross_c, var, *gram_b = tie(cross_c, var, *gram_b)

    total_c = total_c + cross_c.astype(F32)
    gram_c = spread_x(total_c)
    cols_c = jnp.concatenate([cols_c, cols_d], axis=0)

    def unturn(parts):
        twice = jnp.concatenate(parts + parts, axis=0)
        lower = lax.dynamic_slice_in_dim(twice, lax.rem(4 - x_at, 4) * half, rows, 0)
        upper = lax.dynamic_slice_in_dim(twice, lax.rem(6 - x_at, 4) * half, rows, 0)
        return lower, upper

    def mul(gram, cols):
        return jnp.dot(gram, cols, preferred_element_type=F32)

    grams = [unturn(g) for g in (gram_a, gram_b)]
    lower, upper = [sum(mul(g[i], c) for g, c in zip(grams, (cols_a, cols_b))) for i in (0, 1)]
    *gram_c, lower, upper = tie(*gram_c, lower, upper)

    lower_c, upper_c = unturn(gram_c)
    away = (upper + mul(upper_c, cols_c)).astype(BF16)
    prod = lower + mul(lower_c, cols_c)
    term = prod / (batch - 1.0) - mine.astype(F32) * var
    far_own, far_got = swap(away[:, :feats], "yl", 1), swap_both(away[:, feats:])
    near_got = swap(term[:, feats:], "core", 1)

    square = sum(jnp.sum(t * t) for t in (total_a, total_b, total_c))
    differ = first_view.astype(F32) - second_view.astype(F32)
    counted = (lax.axis_index("z") == 0) & (lax.axis_index("yl") == 0)
    var_sq = jnp.where(counted, jnp.sum(var * var), F32(0.0))
    loss = (
        25.0 * jnp.sum(differ * differ) / (batch * total_feats)
        + (0.5 * square / (batch - 1.0) ** 2 - var_sq) / total_feats
    )
    spread = lax.all_to_all(jnp.full((256, 1, 128), loss, F32), AXES, 0, 0, tiled=True)
    loss_value = jnp.sum(spread[:, 0, 0])
    far_own, far_got, near_got, loss_value = tie(far_own, far_got, near_got, loss_value)

    weight = 12.5 * (batch - 1.0) / batch
    kept = term[:, :feats] + far_own.astype(F32) / (batch - 1.0)
    got = near_got + far_got.astype(F32) / (batch - 1.0)
    first_grad = jnp.where(is_zero, kept, got) + weight * differ
    second_grad = jnp.where(is_zero, got, kept) - weight * differ
    return first_grad, second_grad, loss_value


def solution(mesh):
    fine = Mesh(mesh.devices.reshape(SIZES), AXES)
    spec = P(("z", "yl"), ("yh", "x", "core"))
    return jax.shard_map(
        per_device,
        mesh=fine,
        in_specs=(spec, spec),
        out_specs=(spec, spec, P()),
        check_vma=False,
    )
```

```python
import jax
import jax.numpy as jnp
from jax import lax
from jax.sharding import Mesh, PartitionSpec as P

AXES = ("z", "yl", "yh", "x", "core")
SIZES = (8, 2, 2, 4, 2)
F32, BF16 = jnp.float32, jnp.bfloat16


def shift(value, axis, step):
    size = lax.axis_size(axis)
    return lax.ppermute(value, axis, [(i, (i + step) % size) for i in range(size)])


def swap(value, axis, bit):
    size = lax.axis_size(axis)
    return lax.ppermute(value, axis, [(i, i ^ bit) for i in range(size)])


def tie(*values):
    return lax.optimization_barrier(values)


def dot_t(left, right):
    return lax.dot_general(left, right, (((1,), (1,)), ((), ())), preferred_element_type=F32)


def send_x(part):
    block = part.shape[0] // 4
    rounded = part[block:].astype(BF16)
    return [shift(rounded[block * (k - 1) : block * k], "x", k) for k in (1, 2, 3)]


def add_x(part, got):
    total = part[: part.shape[0] // 4]
    for value in got:
        total = total + value.astype(F32)
    return total


def spread_x(total):
    rounded = total.astype(BF16)
    return [rounded] + [shift(rounded, "x", -k) for k in (1, 2, 3)]


def swap_both(value):
    pairs = [(i, i ^ 3) for i in range(4)]
    return lax.ppermute(value, ("yl", "core"), pairs)


def per_device(first_view, second_view):
    rows, feats = first_view.shape
    batch = rows * 16
    total_feats = feats * 16
    half = rows // 2
    is_zero = lax.axis_index("core") == 0
    x_at = lax.axis_index("x")
    own = jnp.where(is_zero, first_view, second_view)
    give = jnp.where(is_zero, second_view, first_view)
    raw = jnp.concatenate([own, swap(give, "core", 1)], axis=1)

    up0, dn0 = shift(raw[:half], "z", 1), shift(raw[half:], "z", -1)
    other = swap(raw, "yl", 1)
    up0, dn0, raw = tie(up0, dn0, raw)

    up1 = shift(jnp.concatenate([raw[half:], up0], axis=0), "z", 1)
    dn1 = shift(jnp.concatenate([raw[:half], dn0], axis=0), "z", -1)
    sums = jnp.sum(raw.astype(F32), axis=0, keepdims=True)
    every = lax.all_to_all(jnp.broadcast_to(sums[None], (16, 1, 2 * feats)), ("z", "yl"), 0, 0, tiled=True)
    mean = jnp.sum(every, axis=0) / batch
    up1, dn1, mean, other = tie(up1, dn1, mean, other)

    def center(value):
        return (value.astype(F32) - mean).astype(BF16)

    def centers(*values):
        return jnp.concatenate([center(v) for v in values], axis=0)

    def mul(gram, cols):
        return jnp.dot(gram, cols, preferred_element_type=F32)

    def unturn(parts):
        def block(j):
            value = parts[(j - 3) % 4]
            for at in (2, 1, 0):
                value = jnp.where(x_at == at, parts[(j - at) % 4], value)
            return value

        return jnp.concatenate([block(j) for j in range(4)], axis=0)

    up2, dn2 = shift(up1, "z", 1), shift(dn1, "z", -1)
    mine = center(raw)
    left = jnp.concatenate([mine, center(other)], axis=0)
    turned = lax.dynamic_slice_in_dim(jnp.concatenate([left, left], axis=0), x_at * half, 2 * rows, 0)
    cols_a = jnp.concatenate([mine, centers(up0, dn0)], axis=0)
    cols_b = centers(up1, dn1)
    part_a = jnp.concatenate([dot_t(turned, cols_a), dot_t(turned, cols_b)], axis=1)
    got_a = send_x(part_a)
    up2, dn2, part_a, *got_a = tie(up2, dn2, part_a, *got_a)

    up3, dn3 = shift(up2, "z", 1), shift(dn2, "z", -1)
    total_a = add_x(part_a, got_a)
    total_a = total_a + swap(total_a.astype(BF16), "yh", 1).astype(F32)
    total_b = total_a[:, 2 * rows :]
    gram_a = spread_x(total_a[:, : 2 * rows])
    cols_c = centers(up2, dn2)
    part_c = dot_t(turned, cols_c)
    got_c = send_x(part_c)
    up3, dn3, total_a, total_b, part_c, *both = tie(up3, dn3, total_a, total_b, part_c, *gram_a, *got_c)
    gram_a, got_c = both[:4], both[4:]

    cols_d = centers(up3, dn3)
    part_d = dot_t(turned, cols_d)
    got_d = send_x(part_d)
    total_c = add_x(part_c, got_c)
    total_b, total_c, part_d, *both = tie(total_b, total_c, part_d, *gram_a, *got_d)
    gram_a, got_d = both[:4], both[4:]

    total_c = jnp.concatenate([total_c, add_x(part_d, got_d)], axis=1)
    cross_c = swap(total_c.astype(BF16), "yh", 1)
    gram_b = spread_x(total_b)
    squares = sum(
        jnp.sum(jnp.square(c.astype(F32)), axis=0, keepdims=True) for c in (cols_a, cols_b, cols_c, cols_d)
    )
    var = (squares + swap(squares, "yl", 1)) / (batch - 1)
    prod = mul(unturn(gram_a), cols_a)
    square = jnp.sum(total_a * total_a)
    differ = first_view.astype(F32) - second_view.astype(F32)
    diff_sq = jnp.sum(differ * differ)
    total_c, cross_c, var, prod, square, diff_sq, *gram_b = tie(
        total_c, cross_c, var, prod, square, diff_sq, *gram_b
    )

    total_c = total_c + cross_c.astype(F32)
    gram_c = spread_x(total_c)
    cols_c = jnp.concatenate([cols_c, cols_d], axis=0)
    prod = prod + mul(unturn(gram_b), cols_b)
    square = square + jnp.sum(total_c * total_c)
    counted = (lax.axis_index("z") == 0) & (lax.axis_index("yl") == 0)
    var_sq = jnp.where(counted, jnp.sum(var * var), F32(0.0))
    loss = (
        25.0 * diff_sq / (batch * total_feats)
        + (0.5 * square / (batch - 1.0) ** 2 - var_sq) / total_feats
    )
    loss = jnp.full((256, 1, 128), loss, F32)
    prod, cols_c, loss, *gram_c = tie(prod, cols_c, loss, *gram_c)

    gram_c = unturn(gram_c)
    away = (prod[rows:] + mul(gram_c[rows:], cols_c)).astype(BF16)
    far_own, far_got = swap(away[:, :feats], "yl", 1), swap_both(away[:, feats:])
    term = (prod[:rows] + mul(gram_c[:rows], cols_c)) / (batch - 1.0) - mine.astype(F32) * var
    near_got = swap(term[:, feats:], "core", 1)
    spread = lax.all_to_all(loss, AXES, 0, 0, tiled=True)
    loss_value = jnp.sum(spread[:, 0, 0])
    far_own, far_got, near_got, loss_value = tie(far_own, far_got, near_got, loss_value)

    weight = 12.5 * (batch - 1.0) / batch
    kept = term[:, :feats] + far_own.astype(F32) / (batch - 1.0)
    got = near_got + far_got.astype(F32) / (batch - 1.0)
    first_grad = jnp.where(is_zero, kept, got) + weight * differ
    second_grad = jnp.where(is_zero, got, kept) - weight * differ
    return first_grad, second_grad, loss_value


def solution(mesh):
    fine = Mesh(mesh.devices.reshape(SIZES), AXES)
    spec = P(("z", "yl"), ("yh", "x", "core"))
    return jax.shard_map(
        per_device,
        mesh=fine,
        in_specs=(spec, spec),
        out_specs=(spec, spec, P()),
        check_vma=False,
    )
```

```python
import jax
import jax.numpy as jnp
from jax import lax
from jax.sharding import Mesh, PartitionSpec as P
AXES = ('z', 'yl', 'yh', 'x', 'core')
SIZES = (8, 2, 2, 4, 2)
F32, BF16 = (jnp.float32, jnp.bfloat16)

def shift(value, axis, step):
    size = lax.axis_size(axis)
    return lax.ppermute(value, axis, [(i, (i + step) % size) for i in range(size)])

def swap(value, axis, bit):
    size = lax.axis_size(axis)
    return lax.ppermute(value, axis, [(i, i ^ bit) for i in range(size)])

def swap_both(value):
    pairs = [(i, i ^ 3) for i in range(4)]
    return lax.ppermute(value, ('yl', 'core'), pairs)

def tie(*values):
    return lax.optimization_barrier(values)

def dot_t(left, right):
    return lax.dot_general(left, right, (((1,), (1,)), ((), ())), preferred_element_type=F32)

def send_x(part):
    size = part.shape[0] // 4
    at = lax.axis_index('x')

    def block(k):
        return lax.dynamic_slice_in_dim(part, lax.rem(at + k, 4) * size, size, 0)
    return (block(0), [shift(block(k).astype(BF16), 'x', k) for k in (1, 2, 3)])

def add_x(own, got):
    total = own
    for value in got:
        total = total + value.astype(F32)
    return total

def spread_x(total):
    rounded = total.astype(BF16)
    return [rounded] + [shift(rounded, 'x', -k) for k in (1, 2, 3)]

def per_device(first_view, second_view):
    rows, feats = first_view.shape
    batch = rows * 16
    total_feats = feats * 16
    half = rows // 2
    is_zero = lax.axis_index('core') == 0
    x_at = lax.axis_index('x')
    own = jnp.where(is_zero, first_view, second_view)
    give = jnp.where(is_zero, second_view, first_view)
    raw = jnp.concatenate([own, swap(give, 'core', 1)], axis=1)

    def center(value):
        return (value.astype(F32) - mean).astype(BF16)

    def centers(*values):
        return jnp.concatenate([center(v) for v in values], axis=0)

    def mul(gram, cols):
        return jnp.dot(gram, cols, preferred_element_type=F32)

    def unturn(parts):

        def block(j):
            value = parts[(j - 3) % 4]
            for at in (2, 1, 0):
                value = jnp.where(x_at == at, parts[(j - at) % 4], value)
            return value
        return jnp.concatenate([block(j) for j in range(4)], axis=0)

    def get_mean(value):
        sums = jnp.sum(value.astype(F32), axis=0, keepdims=True)
        every = lax.all_to_all(jnp.broadcast_to(sums[None], (16, 1, 2 * feats)), ('z', 'yl'), 0, 0, tiled=True)
        return jnp.sum(every, axis=0) / batch
    up0, dn0 = (shift(raw[:half], 'z', 1), shift(raw[half:], 'z', -1))
    mean = get_mean(raw)
    up0, dn0, raw, mean = tie(up0, dn0, raw, mean)
    up1 = shift(jnp.concatenate([raw[half:], up0], axis=0), 'z', 1)
    dn1 = shift(jnp.concatenate([raw[:half], dn0], axis=0), 'z', -1)
    other = swap(raw, 'yl', 1)
    mine = center(raw)
    cols_a = jnp.concatenate([mine, centers(up0, dn0)], axis=0)
    up1, dn1, mean, other, mine, cols_a = tie(up1, dn1, mean, other, mine, cols_a)
    up2, dn2 = (shift(up1, 'z', 1), shift(dn1, 'z', -1))
    left = jnp.concatenate([mine, center(other)], axis=0)
    cols_b = centers(up1, dn1)
    part_a, got_a = send_x(jnp.concatenate([dot_t(left, cols_a), dot_t(left, cols_b)], axis=1))
    up2, dn2, part_a, *got_a = tie(up2, dn2, part_a, *got_a)
    up3, dn3 = (shift(up2, 'z', 1), shift(dn2, 'z', -1))
    total_a = add_x(part_a, got_a)
    total_a = total_a + swap(total_a.astype(BF16), 'yh', 1).astype(F32)
    total_b = total_a[:, 2 * rows:]
    cols_c = centers(up2, dn2)
    part_c, got_c = send_x(dot_t(left, cols_c))
    gram_a = []
    gram_a = spread_x(total_a[:, :2 * rows])
    up3, dn3, total_a, total_b, part_c, *both = tie(up3, dn3, total_a, total_b, part_c, *got_c, *gram_a)
    got_c, gram_a = (both[:3], both[3:])
    cols_d = centers(up3, dn3)
    part_d, got_d = send_x(dot_t(left, cols_d))
    total_c = add_x(part_c, got_c)
    gram_b = []
    total_a, total_b, total_c, part_d, cols_c, cols_d, *both = tie(total_a, total_b, total_c, part_d, cols_c, cols_d, *got_d, *gram_a, *gram_b)
    got_d, gram_a, gram_b = (both[:3], both[3:7], both[7:])
    total_c = jnp.concatenate([total_c, add_x(part_d, got_d)], axis=1)
    cross_c = swap(total_c.astype(BF16), 'yh', 1)
    gram_b = spread_x(total_b)
    prod = []
    prod = [mul(unturn(gram_a), cols_a)]
    late = [cols_c, cols_d]
    late = [jnp.concatenate(late, axis=0)]

    def sums_of(cols):
        return sum((jnp.sum(jnp.square(c.astype(F32)), axis=0, keepdims=True) for c in cols))
    squares = []
    squares = [sums_of((cols_a, cols_b, *late))]
    total_c, cross_c, *both = tie(total_c, cross_c, *gram_a, *gram_b, *late, *squares, *prod)
    gram_a, gram_b, both = (both[:4], both[4:8], both[8:])
    late, both = (both[:len(late)], both[len(late):])
    total_c = total_c + cross_c.astype(F32)
    gram_c = spread_x(total_c)
    prod = both[-1] + mul(unturn(gram_b), cols_b)
    squares = both[0]
    var = (squares + swap(squares, 'yl', 1)) / (batch - 1)
    square = jnp.sum(total_a * total_a) + jnp.sum(total_c * total_c)
    differ = first_view.astype(F32) - second_view.astype(F32)
    counted = (lax.axis_index('z') == 0) & (lax.axis_index('yl') == 0)
    var_sq = jnp.where(counted, jnp.sum(var * var), F32(0.0))
    loss = (25.0 * jnp.sum(differ * differ) / batch - var_sq) / total_feats
    square = square / ((batch - 1.0) ** 2 * total_feats)
    loss = jnp.full((256, 1, 128), loss + 0.5 * square, F32)
    prod, var, loss, *both = tie(prod, var, loss, *gram_c, *late)
    gram_c, late = (both[:4], both[4:])
    gram_c = unturn(gram_c)

    def rest(gram):
        total, at = (None, 0)
        for cols in late:
            value = mul(gram[:, at:at + cols.shape[0]], cols)
            total = value if total is None else total + value
            at += cols.shape[0]
        return total
    away = (prod[rows:] + rest(gram_c[rows:])).astype(BF16)
    lower = gram_c[:rows]
    prod = prod[:rows] + rest(lower)
    far_own, far_got = (swap(away[:, :feats], 'yl', 1), swap_both(away[:, feats:]))
    term = prod / (batch - 1.0) - mine.astype(F32) * var
    near_got = swap(term[:, feats:], 'core', 1)
    spread = lax.all_to_all(loss, AXES, 0, 0, tiled=True)
    loss_value = jnp.sum(spread[:, 0, 0])
    far_own, far_got, near_got, loss_value = tie(far_own, far_got, near_got, loss_value)
    weight = 12.5 * (batch - 1.0) / batch
    kept = term[:, :feats] + far_own.astype(F32) / (batch - 1.0)
    got = near_got + far_got.astype(F32) / (batch - 1.0)
    first_grad = jnp.where(is_zero, kept, got) + weight * differ
    second_grad = jnp.where(is_zero, got, kept) - weight * differ
    return (first_grad, second_grad, loss_value)

def solution(mesh):
    fine = Mesh(mesh.devices.reshape(SIZES), AXES)
    spec = P(('z', 'yl'), ('yh', 'x', 'core'))
    return jax.shard_map(per_device, mesh=fine, in_specs=(spec, spec), out_specs=(spec, spec, P()), check_vma=False)
```

```python
import jax
import jax.numpy as jnp
from jax import lax
from jax.sharding import Mesh, PartitionSpec as P
AXES = ('z', 'yl', 'yh', 'x', 'core')
SIZES = (8, 2, 2, 4, 2)
F32, BF16 = (jnp.float32, jnp.bfloat16)

def shift(value, axis, step):
    size = lax.axis_size(axis)
    return lax.ppermute(value, axis, [(i, (i + step) % size) for i in range(size)])

def swap(value, axis, bit):
    size = lax.axis_size(axis)
    return lax.ppermute(value, axis, [(i, i ^ bit) for i in range(size)])

def swap_both(value):
    pairs = [(i, i ^ 3) for i in range(4)]
    return lax.ppermute(value, ('yl', 'core'), pairs)

def tie(*values):
    return lax.optimization_barrier(values)

def dot_t(left, right):
    return lax.dot_general(left, right, (((1,), (1,)), ((), ())), preferred_element_type=F32)

def send_x(part):
    size = part.shape[0] // 4
    at = lax.axis_index('x')

    def block(k):
        return lax.dynamic_slice_in_dim(part, lax.rem(at + k, 4) * size, size, 0)
    return (block(0), [shift(block(k).astype(BF16), 'x', k) for k in (1, 2, 3)])

def add_x(own, got):
    total = own
    for value in got:
        total = total + value.astype(F32)
    return total

def spread_x(total):
    rounded = total.astype(BF16)
    return [rounded] + [shift(rounded, 'x', -k) for k in (1, 2, 3)]

def relay_one(total):
    rounded = total.astype(BF16)
    return [rounded, shift(rounded, 'x', -1), shift(rounded, 'x', 1)]

def relay_two(parts):
    mine, above, below = parts
    return [mine, above, shift(above, 'x', -1), below]

def per_device(first_view, second_view):
    rows, feats = first_view.shape
    batch = rows * 16
    total_feats = feats * 16
    half = rows // 2
    is_zero = lax.axis_index('core') == 0
    x_at = lax.axis_index('x')
    own = jnp.where(is_zero, first_view, second_view)
    give = jnp.where(is_zero, second_view, first_view)
    raw = jnp.concatenate([own, swap(give, 'core', 1)], axis=1)

    def center(value):
        return (value.astype(F32) - mean).astype(BF16)

    def centers(*values):
        return jnp.concatenate([center(v) for v in values], axis=0)

    def mul(gram, cols):
        return jnp.dot(gram, cols, preferred_element_type=F32)

    def unturn(parts):

        def block(j):
            value = parts[(j - 3) % 4]
            for at in (2, 1, 0):
                value = jnp.where(x_at == at, parts[(j - at) % 4], value)
            return value
        return jnp.concatenate([block(j) for j in range(4)], axis=0)

    def get_mean(value):
        sums = jnp.sum(value.astype(F32), axis=0, keepdims=True)
        every = lax.all_to_all(jnp.broadcast_to(sums[None], (16, 1, 2 * feats)), ('z', 'yl'), 0, 0, tiled=True)
        return jnp.sum(every, axis=0) / batch
    up0, dn0 = (shift(raw[:half], 'z', 1), shift(raw[half:], 'z', -1))
    mean = get_mean(raw)
    up0, dn0, raw, mean = tie(up0, dn0, raw, mean)
    up1 = shift(jnp.concatenate([raw[half:], up0], axis=0), 'z', 1)
    dn1 = shift(jnp.concatenate([raw[:half], dn0], axis=0), 'z', -1)
    other = swap(raw, 'yl', 1)
    mine = center(raw)
    cols_a = jnp.concatenate([mine, centers(up0, dn0)], axis=0)
    up1, dn1, mean, other, mine, cols_a = tie(up1, dn1, mean, other, mine, cols_a)
    up2, dn2 = (shift(up1, 'z', 1), shift(dn1, 'z', -1))
    left = jnp.concatenate([mine, center(other)], axis=0)
    cols_b = centers(up1, dn1)
    part_a, got_a = send_x(jnp.concatenate([dot_t(left, cols_a), dot_t(left, cols_b)], axis=1))
    up2, dn2, part_a, *got_a = tie(up2, dn2, part_a, *got_a)
    up3, dn3 = (shift(up2, 'z', 1), shift(dn2, 'z', -1))
    total_a = add_x(part_a, got_a)
    total_a = total_a + swap(total_a.astype(BF16), 'yh', 1).astype(F32)
    total_b = total_a[:, 2 * rows:]
    cols_c = centers(up2, dn2)
    part_c, got_c = send_x(dot_t(left, cols_c))
    gram_a = []
    gram_a = relay_one(total_a[:, :2 * rows])
    up3, dn3, total_a, total_b, part_c, *both = tie(up3, dn3, total_a, total_b, part_c, *got_c, *gram_a)
    got_c, gram_a = (both[:3], both[3:])
    cols_d = centers(up3, dn3)
    dot_d = dot_t(left, cols_d)
    dot_d, total_b, *gram_a = tie(dot_d, total_b, *gram_a)
    part_d, got_d = send_x(dot_d)
    total_c = add_x(part_c, got_c)
    gram_b = []
    gram_a = relay_two(gram_a)
    gram_b = relay_one(total_b)
    total_a, total_b, total_c, part_d, cols_c, cols_d, *both = tie(total_a, total_b, total_c, part_d, cols_c, cols_d, *got_d, *gram_a, *gram_b)
    got_d, gram_a, gram_b = (both[:3], both[3:7], both[7:])
    total_c = jnp.concatenate([total_c, add_x(part_d, got_d)], axis=1)
    cross_c = swap(total_c.astype(BF16), 'yh', 1)
    gram_b = relay_two(gram_b)
    prod = []
    prod = [mul(unturn(gram_a), cols_a)]
    late = [cols_c, cols_d]
    late = [jnp.concatenate(late, axis=0)]

    def sums_of(cols):
        return sum((jnp.sum(jnp.square(c.astype(F32)), axis=0, keepdims=True) for c in cols))
    squares = []
    squares = [sums_of((cols_a, cols_b, *late))]
    total_c, cross_c, *both = tie(total_c, cross_c, *gram_a, *gram_b, *late, *squares, *prod)
    gram_a, gram_b, both = (both[:4], both[4:8], both[8:])
    late, both = (both[:len(late)], both[len(late):])
    total_c = total_c + cross_c.astype(F32)
    gram_c = spread_x(total_c)
    prod = both[-1] + mul(unturn(gram_b), cols_b)
    squares = both[0]
    var = (squares + swap(squares, 'yl', 1)) / (batch - 1)
    square = jnp.sum(total_a * total_a) + jnp.sum(total_c * total_c)
    differ = first_view.astype(F32) - second_view.astype(F32)
    counted = (lax.axis_index('z') == 0) & (lax.axis_index('yl') == 0)
    var_sq = jnp.where(counted, jnp.sum(var * var), F32(0.0))
    loss = (25.0 * jnp.sum(differ * differ) / batch - var_sq) / total_feats
    square = square / ((batch - 1.0) ** 2 * total_feats)
    loss = jnp.full((256, 1, 128), loss + 0.5 * square, F32)
    prod, var, loss, *both = tie(prod, var, loss, *gram_c, *late)
    gram_c, late = (both[:4], both[4:])
    gram_c = unturn(gram_c)

    def rest(gram):
        total, at = (None, 0)
        for cols in late:
            value = mul(gram[:, at:at + cols.shape[0]], cols)
            total = value if total is None else total + value
            at += cols.shape[0]
        return total
    away = (prod[rows:] + rest(gram_c[rows:])).astype(BF16)
    lower = gram_c[:rows]
    prod = prod[:rows] + rest(lower)
    far_own, far_got = (swap(away[:, :feats], 'yl', 1), swap_both(away[:, feats:]))
    term = prod / (batch - 1.0) - mine.astype(F32) * var
    near = term[:, feats:]
    near_got = swap(near, 'core', 1)
    spread = lax.all_to_all(loss, AXES, 0, 0, tiled=True)
    loss_value = jnp.sum(spread[:, 0, 0])
    far_own, far_got, near_got, loss_value = tie(far_own, far_got, near_got, loss_value)
    weight = 12.5 * (batch - 1.0) / batch
    kept = term[:, :feats] + far_own.astype(F32) / (batch - 1.0)
    got = near_got + far_got.astype(F32) / (batch - 1.0)
    first_grad = jnp.where(is_zero, kept, got) + weight * differ
    second_grad = jnp.where(is_zero, got, kept) - weight * differ
    return (first_grad, second_grad, loss_value)

def solution(mesh):
    fine = Mesh(mesh.devices.reshape(SIZES), AXES)
    spec = P(('z', 'yl'), ('yh', 'x', 'core'))
    return jax.shard_map(per_device, mesh=fine, in_specs=(spec, spec), out_specs=(spec, spec, P()), check_vma=False)
```

```python
import jax
import jax.numpy as jnp
from jax import lax
from jax.sharding import Mesh, PartitionSpec as P
AXES = ('z', 'yl', 'yh', 'x', 'core')
SIZES = (8, 2, 2, 4, 2)
F32, BF16 = (jnp.float32, jnp.bfloat16)

def shift(value, axis, step):
    size = lax.axis_size(axis)
    return lax.ppermute(value, axis, [(i, (i + step) % size) for i in range(size)])

def swap(value, axis, bit):
    size = lax.axis_size(axis)
    return lax.ppermute(value, axis, [(i, i ^ bit) for i in range(size)])

def swap_both(value):
    pairs = [(i, i ^ 3) for i in range(4)]
    return lax.ppermute(value, ('yl', 'core'), pairs)

def tie(*values):
    return lax.optimization_barrier(values)

def dot_t(left, right):
    return lax.dot_general(left, right, (((1,), (1,)), ((), ())), preferred_element_type=F32)

def send_x(part):
    size = part.shape[0] // 4
    at = lax.axis_index('x')

    def block(k):
        return lax.dynamic_slice_in_dim(part, lax.rem(at + k, 4) * size, size, 0)
    return (block(0), [shift(block(k).astype(BF16), 'x', k) for k in (1, 2, 3)])

def add_x(own, got):
    total = own
    for value in got:
        total = total + value.astype(F32)
    return total

def spread_x(total):
    rounded = total.astype(BF16)
    return [rounded] + [shift(rounded, 'x', -k) for k in (1, 2, 3)]

def per_device(first_view, second_view):
    rows, feats = first_view.shape
    batch = rows * 16
    total_feats = feats * 16
    half = rows // 2
    is_zero = lax.axis_index('core') == 0
    x_at = lax.axis_index('x')
    own = jnp.where(is_zero, first_view, second_view)
    give = jnp.where(is_zero, second_view, first_view)
    raw = jnp.concatenate([own, swap(give, 'core', 1)], axis=1)

    def center(value):
        return (value.astype(F32) - mean).astype(BF16)

    def centers(*values):
        return jnp.concatenate([center(v) for v in values], axis=0)

    def mul(gram, cols):
        return jnp.dot(gram, cols, preferred_element_type=F32)

    def unturn(parts):

        def block(j):
            value = parts[(j - 3) % 4]
            for at in (2, 1, 0):
                value = jnp.where(x_at == at, parts[(j - at) % 4], value)
            return value
        return jnp.concatenate([block(j) for j in range(4)], axis=0)

    def get_mean(value):
        sums = jnp.sum(value.astype(F32), axis=0, keepdims=True)
        every = lax.all_to_all(jnp.broadcast_to(sums[None], (16, 1, 2 * feats)), ('z', 'yl'), 0, 0, tiled=True)
        return jnp.sum(every, axis=0) / batch
    up0, dn0 = (shift(raw[:half], 'z', 1), shift(raw[half:], 'z', -1))
    mean = get_mean(raw)
    up0, dn0, raw, mean = tie(up0, dn0, raw, mean)
    up1 = shift(jnp.concatenate([raw[half:], up0], axis=0), 'z', 1)
    dn1 = shift(jnp.concatenate([raw[:half], dn0], axis=0), 'z', -1)
    other = swap(raw, 'yl', 1)
    mine = center(raw)
    cols_a = jnp.concatenate([mine, centers(up0, dn0)], axis=0)
    up1, dn1, mean, other, mine, cols_a = tie(up1, dn1, mean, other, mine, cols_a)
    up2, dn2 = (shift(up1, 'z', 1), shift(dn1, 'z', -1))
    left = jnp.concatenate([mine, center(other)], axis=0)
    cols_b = centers(up1, dn1)
    part_a, got_a = send_x(jnp.concatenate([dot_t(left, cols_a), dot_t(left, cols_b)], axis=1))
    up2, dn2, part_a, *got_a = tie(up2, dn2, part_a, *got_a)
    up3, dn3 = (shift(up2, 'z', 1), shift(dn2, 'z', -1))
    total_a = add_x(part_a, got_a)
    total_a = total_a + swap(total_a.astype(BF16), 'yh', 1).astype(F32)
    total_b = total_a[:, 2 * rows:]
    cols_c = centers(up2, dn2)
    part_c, got_c = send_x(dot_t(left, cols_c))
    gram_a = []
    gram_a = spread_x(total_a[:, :2 * rows])
    up3, dn3, total_a, total_b, part_c, *both = tie(up3, dn3, total_a, total_b, part_c, *got_c, *gram_a)
    got_c, gram_a = (both[:3], both[3:])
    cols_d = centers(up3, dn3)
    dot_d = dot_t(left, cols_d)
    part_d, got_d = send_x(dot_d)
    total_c = add_x(part_c, got_c)
    gram_b = []
    total_a, total_b, total_c, part_d, cols_c, cols_d, *both = tie(total_a, total_b, total_c, part_d, cols_c, cols_d, *got_d, *gram_a, *gram_b)
    got_d, gram_a, gram_b = (both[:3], both[3:7], both[7:])
    total_c = jnp.concatenate([total_c, add_x(part_d, got_d)], axis=1)
    cross_c = swap(total_c.astype(BF16), 'yh', 1)
    gram_b = spread_x(total_b)
    prod = []
    prod = [mul(unturn(gram_a), cols_a)]
    late = [cols_c, cols_d]
    late = [jnp.concatenate(late, axis=0)]

    def sums_of(cols):
        return sum((jnp.sum(jnp.square(c.astype(F32)), axis=0, keepdims=True) for c in cols))
    squares = []
    squares = [sums_of((cols_a, cols_b, *late))]
    total_c, cross_c, *both = tie(total_c, cross_c, *gram_a, *gram_b, *late, *squares, *prod)
    gram_a, gram_b, both = (both[:4], both[4:8], both[8:])
    late, both = (both[:len(late)], both[len(late):])
    total_c = total_c + cross_c.astype(F32)
    gram_c = spread_x(total_c)
    prod = both[-1] + mul(unturn(gram_b), cols_b)
    squares = both[0]
    var = (squares + swap(squares, 'yl', 1)) / (batch - 1)
    square = jnp.sum(total_a * total_a) + jnp.sum(total_c * total_c)
    differ = first_view.astype(F32) - second_view.astype(F32)
    counted = (lax.axis_index('z') == 0) & (lax.axis_index('yl') == 0)
    var_sq = jnp.where(counted, jnp.sum(var * var), F32(0.0))
    loss = (25.0 * jnp.sum(differ * differ) / batch - var_sq) / total_feats
    square = square / ((batch - 1.0) ** 2 * total_feats)
    loss = jnp.full((1, 128), loss + 0.5 * square, F32)
    loss = loss + swap(loss, 'core', 1)
    loss = jnp.broadcast_to(loss[None], (128, 1, 128))
    prod, var, loss, *both = tie(prod, var, loss, *gram_c, *late)
    gram_c, late = (both[:4], both[4:])
    gram_c = unturn(gram_c)

    def rest(gram):
        total, at = (None, 0)
        for cols in late:
            value = mul(gram[:, at:at + cols.shape[0]], cols)
            total = value if total is None else total + value
            at += cols.shape[0]
        return total
    away = (prod[rows:] + rest(gram_c[rows:])).astype(BF16)
    lower = gram_c[:rows]
    away, lower = tie(away, lower)
    prod = prod[:rows] + rest(lower)
    far_own, far_got = (swap(away[:, :feats], 'yl', 1), swap_both(away[:, feats:]))
    term = prod / (batch - 1.0) - mine.astype(F32) * var
    near = term[:, feats:]
    near_got = swap(near, 'core', 1)
    spread = lax.all_to_all(loss, {'zxc': ('z', 'x', 'core'), 'zyx': AXES[:4]}.get('zyx', AXES), 0, 0, tiled=True)
    loss_value = jnp.sum(spread[:, 0, 0])
    far_own, far_got, near_got, loss_value = tie(far_own, far_got, near_got, loss_value)
    weight = 12.5 * (batch - 1.0) / batch
    kept = term[:, :feats] + far_own.astype(F32) / (batch - 1.0)
    got = near_got + far_got.astype(F32) / (batch - 1.0)
    first_grad = jnp.where(is_zero, kept, got) + weight * differ
    second_grad = jnp.where(is_zero, got, kept) - weight * differ
    return (first_grad, second_grad, loss_value)

def solution(mesh):
    fine = Mesh(mesh.devices.reshape(SIZES), AXES)
    spec = P(('z', 'yl'), ('yh', 'x', 'core'))
    return jax.shard_map(per_device, mesh=fine, in_specs=(spec, spec), out_specs=(spec, spec, P()), check_vma=False)
```
